512 devices in a mesh: row: 16 (over x, y), col: 32 (over z, core).
Axes of the slice: x: 4, y: 4, z: 16, core: 2. Of those that a mesh axis runs over, the one named last changes fastest.
Arguments:
- species: float32 [512, 256, 2048], P(None, 'col', 'row'), may hold values from -26 to 26, as said below
- start_basis: float32 [512, 256], replicated, may hold values from -6 to 6
Outputs:
- core_fibers: float32 [256, 256, 2048], P('row', 'col')
- basis: float32 [512, 256], replicated
The draws below stay inside these ranges and needn't reach their ends.
Inputs may be any that keep to these rules, and one draw needn't show every extreme that they name: `species`: entries of the slab.
All inputs are finite; a program needn't handle non-finite values.
Results may differ from the reference program's by a relative error of at most 0.00019.
Values sent between devices are 32-bit elements; how exact they have to be, the bound alone decides.
No kernel may reach another device: no remote copies, remote signals or barrier semaphores. Data moves between devices by JAX's collectives and lax.ppermute only.
A program may use at most 64 MiB of HBM per device.

```python
import math
import jax
import jax.numpy as jnp
from jax import lax

NX = 512
RANK = 256
ITERS = 2
NY = 2048
NZ = 256


def draw_species(key, part):
    key = jax.random.fold_in(key, 11)
    keys = jax.random.split(key, 4)
    noise = jnp.clip(jax.random.normal(keys[0], (NX + 2, NZ, NY), jnp.float32), -6.0, 6.0)
    scales = jnp.exp(jax.random.uniform(keys[1], (NX, 1, 1), jnp.float32, 0.0, math.log(2.5)))
    nearby = jax.random.uniform(keys[2], (NX, 1, 1), jnp.float32, -0.35, 0.35)
    farther = jax.random.uniform(keys[3], (NX, 1, 1), jnp.float32, -0.35, 0.35)
    return scales * (noise[:NX] + nearby * noise[1:NX + 1] + farther * noise[2:NX + 2])


def scatter_about(stream_key, shape, spread, limit, held_as=jnp.bfloat16):
    drawn = spread * jax.random.normal(stream_key, shape, jnp.float32)
    return jnp.clip(drawn, min=-limit, max=limit).astype(held_as)


def setup_inputs(seed: int = 0) -> dict:
    key_of = jax.random.split(jax.random.key(seed), 3)
    species = draw_species(jax.random.fold_in(key_of[2], 71), 0)
    start_basis = scatter_about(key_of[1], (NX, RANK), 1.0, 6.0, jnp.float32)
    return dict(species=species, start_basis=start_basis)


def power_steps(tri_lower, start_basis):
    current = start_basis
    for sweep_number in range(ITERS):
        halfway = jnp.dot(tri_lower.T.astype(jnp.float32), current.astype(jnp.float32), precision=lax.Precision.HIGHEST, preferred_element_type=jnp.float32)
        applied = jnp.dot(tri_lower.astype(jnp.float32), halfway.astype(jnp.float32), precision=lax.Precision.HIGHEST, preferred_element_type=jnp.float32)
        inner_gram = jnp.dot(applied.T.astype(jnp.float32), applied.astype(jnp.float32), precision=lax.Precision.HIGHEST, preferred_element_type=jnp.float32)
        small_lower = jnp.linalg.cholesky(inner_gram)
        current = jax.scipy.linalg.solve_triangular(small_lower, applied.T, lower=True).T
    return current

def reference(species, start_basis):
    unfolded = species.reshape(NX, NZ * NY)
    gram = jnp.dot(unfolded.astype(jnp.float32), unfolded.T.astype(jnp.float32), precision=lax.Precision.HIGHEST, preferred_element_type=jnp.float32)
    tri_lower = jnp.linalg.cholesky(gram)
    basis = power_steps(tri_lower, start_basis)
    core_flat = jnp.dot(basis.T.astype(jnp.float32), unfolded.astype(jnp.float32), precision=lax.Precision.HIGHEST, preferred_element_type=jnp.float32)
    return (core_flat.reshape(RANK, NZ, NY), basis)
```

```python
import jax
import jax.numpy as jnp
from jax import lax
from jax.experimental import pallas as pl
from jax.experimental.pallas import tpu as pltpu
from jax.sharding import Mesh, PartitionSpec as P

ITERS = 2
TILE = 128
PANEL = 8
NT = (((1,), (1,)), ((), ()))
NN = (((1,), (0,)), ((), ()))
PARAMS = pltpu.CompilerParams(vmem_limit_bytes=40 * 2**20)


def matmul(left, right, dims=NN):
    return lax.dot_general(
        left, right, dims, precision=lax.Precision.HIGHEST, preferred_element_type=jnp.float32
    )


def halves(value):
    high = value.astype(jnp.bfloat16)
    return high, (value - high.astype(jnp.float32)).astype(jnp.bfloat16)


def dot16(left, right, dims):
    return lax.dot_general(left, right, dims, preferred_element_type=jnp.float32)


def lower_tiles(count):
    return [(i, j) for i in range(count) for j in range(i + 1)]


def gram_kernel(x_ref, packed_ref, high_ref, low_ref):
    width, cells_z, cells_y = x_ref.shape
    flat = x_ref.reshape(width * cells_z, cells_y)
    for z in range(cells_z):
        high, low = halves(flat[pl.ds(z, width, stride=cells_z), :])
        high_ref[:, z * cells_y : (z + 1) * cells_y] = high
        low_ref[:, z * cells_y : (z + 1) * cells_y] = low
    side = 2 * TILE
    for i, j in lower_tiles(width // side):
        rows, columns = pl.ds(i * side, side), pl.ds(j * side, side)
        block = dot16(high_ref[rows, :], high_ref[columns, :], NT)
        cross = dot16(high_ref[rows, :], low_ref[columns, :], NT)
        if i == j:
            block = block + (cross + cross.T)
        else:
            block = block + (cross + dot16(low_ref[rows, :], high_ref[columns, :], NT))
        for place, (a, b) in enumerate(lower_tiles(width // TILE)):
            if (a // 2, b // 2) == (i, j):
                ra, rb = (a % 2) * TILE, (b % 2) * TILE
                packed_ref[place * TILE : (place + 1) * TILE, :] = block[ra : ra + TILE, rb : rb + TILE]


def spread_row(tile, k):
    return jnp.broadcast_to(tile[k : k + 1, :], tile.shape)


def spread_column(tile, k):
    return jnp.broadcast_to(tile[:, k : k + 1], tile.shape)


def inverse_factor(matrix):
    size = matrix.shape[0]
    count = size // PANEL
    tiles = [matrix[PANEL * t : PANEL * (t + 1), :] for t in range(count)]
    sub = lax.broadcasted_iota(jnp.int32, (PANEL, size), 0)
    lane = lax.broadcasted_iota(jnp.int32, (PANEL, size), 1)
    done = []
    for t in range(count):
        first = PANEL * t
        panel = (lane >= first) & (lane < first + PANEL)
        columns = [spread_column(tiles[t], first + k) for k in range(PANEL)]
        rest = jnp.where(panel, jnp.where(lane - first == sub, 1.0, 0.0), tiles[t])
        forward, pivots = rest, columns[0]
        for k in range(PANEL):
            here = sub == k
            reciprocal = 1.0 / spread_row(columns[k], k)
            if k:
                forward = jnp.where(sub >= k, rest, forward)
                pivots = jnp.where(here, columns[k], pivots)
            for j in range(k + 1, PANEL):
                scaled = spread_row(columns[j], k) * reciprocal
                columns[j] = jnp.where(here, scaled, columns[j] - columns[k] * scaled)
            scaled = spread_row(rest, k) * reciprocal
            rest = jnp.where(here, scaled, rest - columns[k] * scaled)
        done.append(jnp.where(lane <= first + sub, forward * lax.rsqrt(pivots), 0.0))
        rows = [spread_row(rest, k) for k in range(PANEL)]
        for i in range(t + 1, count):
            total = jnp.where(panel, 0.0, tiles[i])
            for k in range(PANEL):
                total = total - spread_column(tiles[i], first + k) * rows[k]
            tiles[i] = total
    return jnp.concatenate(done, axis=0)


def orthonormal(applied_t):
    half = applied_t.shape[0] // 2
    inner = matmul(applied_t, applied_t, NT)
    inverse_a = inverse_factor(inner[:half, :half])
    below = matmul(inner[half:, :half], inverse_a, NT)
    inverse_b = inverse_factor(inner[half:, half:] - matmul(below, below, NT))
    first = matmul(inverse_a, applied_t[:half])
    second = matmul(inverse_b, applied_t[half:] - matmul(below, first))
    return jnp.concatenate([first, second], axis=0)


def basis_kernel(packed_ref, start_ref, high_ref, low_ref, core_ref, basis_ref, gram_ref):
    width = start_ref.shape[0]
    rank, cells_z, cells_y = core_ref.shape
    for place, (a, b) in enumerate(lower_tiles(width // TILE)):
        tile = packed_ref[place * TILE : (place + 1) * TILE, :]
        gram_ref[a * TILE : (a + 1) * TILE, b * TILE : (b + 1) * TILE] = tile
        if a != b:
            gram_ref[b * TILE : (b + 1) * TILE, a * TILE : (a + 1) * TILE] = tile.T
    current_t = start_ref[...].T
    for sweep_number in range(ITERS):
        current_t = orthonormal(matmul(current_t, gram_ref[...]))
    basis_ref[...] = current_t.T
    high, low = halves(current_t)
    flat = core_ref.reshape(rank * cells_z, cells_y)
    for z in range(0, cells_z, 2):
        columns = pl.ds(z * cells_y, 2 * cells_y)
        block = dot16(high, high_ref[:, columns], NN) + (
            dot16(high, low_ref[:, columns], NN) + dot16(low, high_ref[:, columns], NN)
        )
        flat[pl.ds(z, rank, stride=cells_z), :] = block[:, :cells_y]
        flat[pl.ds(z + 1, rank, stride=cells_z), :] = block[:, cells_y:]


def exchange(value, axes):
    return lax.all_to_all(value, axes, split_axis=0, concat_axis=0, tiled=True)


def sum_over(value, axes, members):
    return exchange(jnp.broadcast_to(value, (members, *value.shape)), axes).sum(axis=0)


def shards(species, start_basis):
    width, cells_z, cells_y = species.shape
    rank = start_basis.shape[1]
    tiles = len(lower_tiles(width // TILE))
    packed, high, low = pl.pallas_call(
        gram_kernel,
        out_shape=(
            jax.ShapeDtypeStruct((tiles * TILE, TILE), jnp.float32),
            jax.ShapeDtypeStruct((width, cells_z * cells_y), jnp.bfloat16),
            jax.ShapeDtypeStruct((width, cells_z * cells_y), jnp.bfloat16),
        ),
        compiler_params=PARAMS,
        name="gram",
    )(species)
    plane = ("row", "core")
    members = lax.axis_size(plane)
    part = exchange(packed.reshape(members, -1, TILE), plane).sum(axis=0)
    part = sum_over(part, "zl", lax.axis_size("zl"))
    part = sum_over(part, "zh", lax.axis_size("zh"))
    packed = exchange(jnp.broadcast_to(part, (members, *part.shape)), plane)
    core, basis = pl.pallas_call(
        basis_kernel,
        out_shape=(
            jax.ShapeDtypeStruct((rank, cells_z, cells_y), jnp.float32),
            jax.ShapeDtypeStruct((width, rank), jnp.float32),
        ),
        scratch_shapes=[pltpu.VMEM((width, width), jnp.float32)],
        compiler_params=PARAMS,
        name="basis",
    )(packed.reshape(-1, TILE), start_basis, high, low)
    core = lax.all_to_all(core, "row", split_axis=0, concat_axis=2, tiled=True)
    return core, basis


def solution(mesh):
    rows, columns = mesh.devices.shape
    fine = Mesh(mesh.devices.reshape(rows, columns // 8, 4, 2), ("row", "zh", "zl", "core"))
    split = ("zh", "zl", "core")
    return jax.shard_map(
        shards,
        mesh=fine,
        in_specs=(P(None, split, "row"), P()),
        out_specs=(P("row", split, None), P()),
        check_vma=False,
    )
```

```python
import jax
import jax.numpy as jnp
from jax import lax
from jax.experimental import pallas as pl
from jax.experimental.pallas import tpu as pltpu
from jax.sharding import Mesh, PartitionSpec as P

ITERS = 2
TILE = 128
SUB = 8
NEAR = 2
NT = (((1,), (1,)), ((), ()))
NN = (((1,), (0,)), ((), ()))
PARAMS = pltpu.CompilerParams(vmem_limit_bytes=40 * 2**20)


def matmul(left, right, dims=NN):
    return lax.dot_general(
        left, right, dims, precision=lax.Precision.HIGHEST, preferred_element_type=jnp.float32
    )


def halves(value):
    high = value.astype(jnp.bfloat16)
    return high, (value - high.astype(jnp.float32)).astype(jnp.bfloat16)


def dot16(left, right, dims):
    return lax.dot_general(left, right, dims, preferred_element_type=jnp.float32)


def product(left, right):
    left_high, left_low = halves(left)
    right_high, right_low = halves(right)
    return dot16(left_high, right_high, NN) + (
        dot16(left_high, right_low, NN) + dot16(left_low, right_high, NN)
    )


def lower_tiles(count):
    return [(i, j) for i in range(count) for j in range(i + 1)]


def gram_kernel(x_ref, packed_ref, high_ref, low_ref):
    width, cells_z, cells_y = x_ref.shape
    flat = x_ref.reshape(width * cells_z, cells_y)
    for z in range(cells_z):
        high, low = halves(flat[pl.ds(z, width, stride=cells_z), :])
        high_ref[:, z * cells_y : (z + 1) * cells_y] = high
        low_ref[:, z * cells_y : (z + 1) * cells_y] = low
    side = 2 * TILE
    for i, j in lower_tiles(width // side):
        rows, columns = pl.ds(i * side, side), pl.ds(j * side, side)
        block = dot16(high_ref[rows, :], high_ref[columns, :], NT)
        cross = dot16(high_ref[rows, :], low_ref[columns, :], NT)
        if i == j:
            block = block + (cross + cross.T)
        else:
            block = block + (cross + dot16(low_ref[rows, :], high_ref[columns, :], NT))
        for place, (a, b) in enumerate(lower_tiles(width // TILE)):
            if (a // 2, b // 2) == (i, j):
                ra, rb = (a % 2) * TILE, (b % 2) * TILE
                packed_ref[place * TILE : (place + 1) * TILE, :] = block[ra : ra + TILE, rb : rb + TILE]


def spread_row(tile, k):
    return jnp.broadcast_to(tile[k : k + 1, :], tile.shape)


def spread_column(tile, k):
    return jnp.broadcast_to(tile[:, k : k + 1], tile.shape)


def total_of(terms):
    while len(terms) > 1:
        terms = [sum(terms[i + 1 : i + 2], terms[i]) for i in range(0, len(terms), 2)]
    return terms[0]


def inverse_factors(matrices, depth):
    size = matrices[0].shape[0]
    count = size // SUB
    sub = lax.broadcasted_iota(jnp.int32, (SUB, size), 0)
    lane = lax.broadcasted_iota(jnp.int32, (SUB, size), 1)
    zero = jnp.zeros((SUB, size), jnp.float32)
    all_tiles = [[m[SUB * t : SUB * (t + 1), :] for t in range(count)] for m in matrices]
    all_done = [[] for _ in matrices]
    for t in range(0, count, depth):
        first, across = SUB * t, SUB * depth
        panel = (lane >= first) & (lane < first + across)
        for tiles, done in zip(all_tiles, all_done):
            own = range(depth)
            columns = [
                [spread_column(tiles[t + q], first + k) for k in range(across)] for q in own
            ]
            rest = [
                jnp.where(
                    panel, jnp.where(lane - first - SUB * q == sub, 1.0, 0.0), tiles[t + q]
                )
                for q in own
            ]
            forward, pivots, scales = list(rest), [None] * depth, [None] * depth
            for k in range(across):
                p, row = divmod(k, SUB)
                here = sub == row
                scale = 1.0 / spread_row(columns[p][k], row)
                factors = [columns[q][k] for q in own]
                factors[p] = jnp.where(here, 0.0, factors[p])
                if row:
                    forward[p] = jnp.where(sub >= row, rest[p], forward[p])
                    pivots[p] = jnp.where(here, columns[p][k], pivots[p])
                    scales[p] = jnp.where(here, scale, scales[p])
                else:
                    forward[p], pivots[p], scales[p] = rest[p], columns[p][k], scale
                for j in range(k + 1, across):
                    spread = spread_row(columns[p][j], row)
                    for q in own:
                        columns[q][j] = columns[q][j] - (factors[q] * spread) * scale
                spread = spread_row(rest[p], row)
                for q in own:
                    rest[q] = rest[q] - (factors[q] * spread) * scale
            solved = [rest[q] * scales[q] for q in own]
            rows = [spread_row(solved[k // SUB], k % SUB) for k in range(across)]
            near = t + depth
            far = min(near + NEAR, count)
            for i in range(near, far):
                change = [spread_column(tiles[i], first + k) * rows[k] for k in range(across)]
                tiles[i] = jnp.where(panel, 0.0, tiles[i]) - total_of(change)
            for q in own:
                kept = lane <= first + SUB * q + sub
                done.append(jnp.where(kept, forward[q] * lax.rsqrt(pivots[q]), 0.0))
            if far < count:
                right = [solved[i - t] if i - t in own else zero for i in range(count)]
                change = matmul(jnp.concatenate(tiles[far:], 0), jnp.concatenate(right, 0))
                for i in range(far, count):
                    place = SUB * (i - far)
                    tiles[i] = jnp.where(panel, 0.0, tiles[i]) - change[place : place + SUB]
    return [jnp.concatenate(done, axis=0) for done in all_done]


def basis_kernel(
    packed_ref, start_ref, high_ref, low_ref, core_ref, basis_ref, *scratch
):
    gram_high, gram_low, current_ref, applied_ref, rest_ref = scratch
    width = start_ref.shape[0]
    rank, cells_z, cells_y = core_ref.shape
    half = rank // 2
    for place, (a, b) in enumerate(lower_tiles(width // TILE)):
        tile = packed_ref[place * TILE : (place + 1) * TILE, :]
        for i, j, value in ((a, b, tile), (b, a, tile.T))[: 1 + (a != b)]:
            rows, columns = pl.ds(i * TILE, TILE), pl.ds(j * TILE, TILE)
            gram_high[rows, columns], gram_low[rows, columns] = halves(value)

    def times_gram(sweep, part):
        high, low = halves(current_ref[sweep, part])
        applied_ref[sweep, part] = dot16(high, gram_high[...], NN) + (
            dot16(high, gram_low[...], NN) + dot16(low, gram_high[...], NN)
        )

    def inner(sweep, left, right):
        return matmul(applied_ref[sweep, left], applied_ref[sweep, right], NT)

    def first_half(sweep, inverse):
        current_ref[sweep + 1, 0] = product(inverse, applied_ref[sweep, 0])

    def second_matrix(sweep, inverse):
        below = matmul(inner(sweep, 1, 0), inverse, NT)
        rest_ref[sweep] = applied_ref[sweep, 1] - matmul(below, current_ref[sweep + 1, 0])
        return inner(sweep, 1, 1) - matmul(below, below, NT)

    def second_half(sweep, inverse):
        current_ref[sweep + 1, 1] = product(inverse, rest_ref[sweep])

    def write(part):
        value = current_ref[ITERS, part]
        basis_ref[:, part * half : (part + 1) * half] = value.T
        high, low = halves(value)
        flat = core_ref.reshape(rank * cells_z, cells_y)
        for z in range(0, cells_z, 2):
            columns = pl.ds(z * cells_y, 2 * cells_y)
            block = dot16(high, high_ref[:, columns], NN) + (
                dot16(high, low_ref[:, columns], NN) + dot16(low, high_ref[:, columns], NN)
            )
            for q in range(2):
                rows = pl.ds(part * half * cells_z + z + q, half, stride=cells_z)
                flat[rows, :] = block[:, q * cells_y : (q + 1) * cells_y]

    for part in range(2):
        current_ref[0, part] = start_ref[:, part * half : (part + 1) * half].T
        times_gram(0, part)
    (inverse,) = inverse_factors([inner(0, 0, 0)], 2)
    for sweep in range(ITERS):
        first_half(sweep, inverse)
        matrix = second_matrix(sweep, inverse)
        if sweep + 1 < ITERS:
            times_gram(sweep + 1, 0)
            second, inverse = inverse_factors([matrix, inner(sweep + 1, 0, 0)], 1)
            second_half(sweep, second)
            times_gram(sweep + 1, 1)
        else:
            write(0)
            (second,) = inverse_factors([matrix], 2)
            second_half(sweep, second)
            write(1)


def exchange(value, axes):
    return lax.all_to_all(value, axes, split_axis=0, concat_axis=0, tiled=True)


def sum_over(value, axes, members):
    return exchange(jnp.broadcast_to(value, (members, *value.shape)), axes).sum(axis=0)


def shards(species, start_basis):
    width, cells_z, cells_y = species.shape
    rank = start_basis.shape[1]
    tiles = len(lower_tiles(width // TILE))
    packed, high, low = pl.pallas_call(
        gram_kernel,
        out_shape=(
            jax.ShapeDtypeStruct((tiles * TILE, TILE), jnp.float32),
            jax.ShapeDtypeStruct((width, cells_z * cells_y), jnp.bfloat16),
            jax.ShapeDtypeStruct((width, cells_z * cells_y), jnp.bfloat16),
        ),
        compiler_params=PARAMS,
        name="gram",
    )(species)
    plane = ("row", "core")
    members = lax.axis_size(plane)
    part = exchange(packed.reshape(members, -1, TILE), plane).sum(axis=0)
    part = sum_over(part, ("zh", "zl"), lax.axis_size(("zh", "zl")))
    packed = exchange(jnp.broadcast_to(part, (members, *part.shape)), plane)
    core, basis = pl.pallas_call(
        basis_kernel,
        out_shape=(
            jax.ShapeDtypeStruct((rank, cells_z, cells_y), jnp.float32),
            jax.ShapeDtypeStruct((width, rank), jnp.float32),
        ),
        scratch_shapes=[
            pltpu.VMEM((width, width), jnp.bfloat16),
            pltpu.VMEM((width, width), jnp.bfloat16),
            pltpu.VMEM((ITERS + 1, 2, rank // 2, width), jnp.float32),
            pltpu.VMEM((ITERS, 2, rank // 2, width), jnp.float32),
            pltpu.VMEM((ITERS, rank // 2, width), jnp.float32),
        ],
        compiler_params=PARAMS,
        name="basis",
    )(packed.reshape(-1, TILE), start_basis, high, low)
    core = lax.all_to_all(core, "row", split_axis=0, concat_axis=2, tiled=True)
    return core, basis


def solution(mesh):
    rows, columns = mesh.devices.shape
    fine = Mesh(mesh.devices.reshape(rows, columns // 8, 4, 2), ("row", "zh", "zl", "core"))
    split = ("zh", "zl", "core")
    return jax.shard_map(
        shards,
        mesh=fine,
        in_specs=(P(None, split, "row"), P()),
        out_specs=(P("row", split, None), P()),
        check_vma=False,
    )
```

```python
import jax
import jax.numpy as jnp
from jax import lax
from jax.experimental import pallas as pl
from jax.experimental.pallas import tpu as pltpu
from jax.sharding import Mesh, PartitionSpec as P

ITERS = 2
TILE = 128
SUB = 8
NEAR = 2
NT = (((1,), (1,)), ((), ()))
NN = (((1,), (0,)), ((), ()))
PARAMS = pltpu.CompilerParams(vmem_limit_bytes=40 * 2**20)


def halves(value):
    high = value.astype(jnp.bfloat16)
    return high, (value - high.astype(jnp.float32)).astype(jnp.bfloat16)


def dot16(left, right, dims):
    return lax.dot_general(left, right, dims, preferred_element_type=jnp.float32)


def matmul(left, right, dims=NN):
    left_high, left_low = halves(left)
    right_high, right_low = halves(right)
    return dot16(left_high, right_high, dims) + (
        dot16(left_high, right_low, dims) + dot16(left_low, right_high, dims)
    )


def lower_tiles(count):
    return [(i, j) for i in range(count) for j in range(i + 1)]


def gram_kernel(x_ref, packed_ref, high_ref, low_ref):
    width, cells_z, cells_y = x_ref.shape
    flat = x_ref.reshape(width * cells_z, cells_y)
    for z in range(cells_z):
        high, low = halves(flat[pl.ds(z, width, stride=cells_z), :])
        high_ref[:, z * cells_y : (z + 1) * cells_y] = high
        low_ref[:, z * cells_y : (z + 1) * cells_y] = low
    side = 2 * TILE
    for i, j in lower_tiles(width // side):
        rows, columns = pl.ds(i * side, side), pl.ds(j * side, side)
        block = dot16(high_ref[rows, :], high_ref[columns, :], NT)
        cross = dot16(high_ref[rows, :], low_ref[columns, :], NT)
        if i == j:
            block = block + (cross + cross.T)
        else:
            block = block + (cross + dot16(low_ref[rows, :], high_ref[columns, :], NT))
        for place, (a, b) in enumerate(lower_tiles(width // TILE)):
            if (a // 2, b // 2) == (i, j):
                ra, rb = (a % 2) * TILE, (b % 2) * TILE
                packed_ref[place * TILE : (place + 1) * TILE, :] = block[ra : ra + TILE, rb : rb + TILE]


def spread_row(tile, k):
    return jnp.broadcast_to(tile[k : k + 1, :], tile.shape)


def spread_column(tile, k):
    return jnp.broadcast_to(tile[:, k : k + 1], tile.shape)


def total_of(terms):
    while len(terms) > 1:
        terms = [sum(terms[i + 1 : i + 2], terms[i]) for i in range(0, len(terms), 2)]
    return terms[0]


def inverse_factors(matrices, depth):
    size = matrices[0].shape[0]
    count = size // SUB
    sub = lax.broadcasted_iota(jnp.int32, (SUB, size), 0)
    lane = lax.broadcasted_iota(jnp.int32, (SUB, size), 1)
    zero = jnp.zeros((SUB, size), jnp.float32)
    all_tiles = [[m[SUB * t : SUB * (t + 1), :] for t in range(count)] for m in matrices]
    all_done = [[] for _ in matrices]
    for t in range(0, count, depth):
        first, across = SUB * t, SUB * depth
        panel = (lane >= first) & (lane < first + across)
        for tiles, done in zip(all_tiles, all_done):
            own = range(depth)
            columns = [
                [spread_column(tiles[t + q], first + k) for k in range(across)] for q in own
            ]
            rest = [
                jnp.where(
                    panel, jnp.where(lane - first - SUB * q == sub, 1.0, 0.0), tiles[t + q]
                )
                for q in own
            ]
            forward, pivots, scales = list(rest), [None] * depth, [None] * depth
            for k in range(across):
                p, row = divmod(k, SUB)
                here = sub == row
                scale = 1.0 / spread_row(columns[p][k], row)
                factors = [columns[q][k] for q in own]
                factors[p] = jnp.where(here, 0.0, factors[p])
                if row:
                    forward[p] = jnp.where(sub >= row, rest[p], forward[p])
                    pivots[p] = jnp.where(here, columns[p][k], pivots[p])
                    scales[p] = jnp.where(here, scale, scales[p])
                else:
                    forward[p], pivots[p], scales[p] = rest[p], columns[p][k], scale
                for j in range(k + 1, across):
                    spread = spread_row(columns[p][j], row)
                    for q in own:
                        columns[q][j] = columns[q][j] - (factors[q] * spread) * scale
                spread = spread_row(rest[p], row)
                for q in own:
                    rest[q] = rest[q] - (factors[q] * spread) * scale
            solved = [rest[q] * scales[q] for q in own]
            rows = [spread_row(solved[k // SUB], k % SUB) for k in range(across)]
            near = t + depth
            far = min(near + NEAR, count)
            for i in range(near, far):
                change = [spread_column(tiles[i], first + k) * rows[k] for k in range(across)]
                tiles[i] = jnp.where(panel, 0.0, tiles[i]) - total_of(change)
            for q in own:
                kept = lane <= first + SUB * q + sub
                done.append(jnp.where(kept, forward[q] * lax.rsqrt(pivots[q]), 0.0))
            if far < count:
                right = [solved[i - t] if i - t in own else zero for i in range(count)]
                change = matmul(jnp.concatenate(tiles[far:], 0), jnp.concatenate(right, 0))
                for i in range(far, count):
                    place = SUB * (i - far)
                    tiles[i] = jnp.where(panel, 0.0, tiles[i]) - change[place : place + SUB]
    return [jnp.concatenate(done, axis=0) for done in all_done]


def basis_kernel(
    packed_ref, start_ref, high_ref, low_ref, core_ref, basis_ref, *scratch
):
    gram_high, gram_low, current_ref, applied_ref, rest_ref = scratch
    width = start_ref.shape[0]
    rank, cells_z, cells_y = core_ref.shape
    half = rank // 2
    for place, (a, b) in enumerate(lower_tiles(width // TILE)):
        tile = packed_ref[place * TILE : (place + 1) * TILE, :]
        for i, j, value in ((a, b, tile), (b, a, tile.T))[: 1 + (a != b)]:
            rows, columns = pl.ds(i * TILE, TILE), pl.ds(j * TILE, TILE)
            gram_high[rows, columns], gram_low[rows, columns] = halves(value)

    def times_gram(sweep, part):
        high, low = halves(current_ref[sweep, part])
        applied_ref[sweep, part] = dot16(high, gram_high[...], NN) + (
            dot16(high, gram_low[...], NN) + dot16(low, gram_high[...], NN)
        )

    def inner(sweep, left, right):
        return matmul(applied_ref[sweep, left], applied_ref[sweep, right], NT)

    def first_half(sweep, inverse):
        current_ref[sweep + 1, 0] = matmul(inverse, applied_ref[sweep, 0])

    def second_matrix(sweep, inverse):
        below = matmul(inner(sweep, 1, 0), inverse, NT)
        rest_ref[sweep] = applied_ref[sweep, 1] - matmul(below, current_ref[sweep + 1, 0])
        return inner(sweep, 1, 1) - matmul(below, below, NT)

    def second_half(sweep, inverse):
        current_ref[sweep + 1, 1] = matmul(inverse, rest_ref[sweep])

    def write(part):
        value = current_ref[ITERS, part]
        basis_ref[:, part * half : (part + 1) * half] = value.T
        high, low = halves(value)
        flat = core_ref.reshape(rank * cells_z, cells_y)
        for z in range(0, cells_z, 2):
            columns = pl.ds(z * cells_y, 2 * cells_y)
            block = dot16(high, high_ref[:, columns], NN) + (
                dot16(high, low_ref[:, columns], NN) + dot16(low, high_ref[:, columns], NN)
            )
            for q in range(2):
                rows = pl.ds(part * half * cells_z + z + q, half, stride=cells_z)
                flat[rows, :] = block[:, q * cells_y : (q + 1) * cells_y]

    for part in range(2):
        current_ref[0, part] = start_ref[:, part * half : (part + 1) * half].T
        times_gram(0, part)
    (inverse,) = inverse_factors([inner(0, 0, 0)], 2)
    for sweep in range(ITERS):
        first_half(sweep, inverse)
        matrix = second_matrix(sweep, inverse)
        if sweep + 1 < ITERS:
            times_gram(sweep + 1, 0)
            second, inverse = inverse_factors([matrix, inner(sweep + 1, 0, 0)], 2)
            second_half(sweep, second)
            times_gram(sweep + 1, 1)
        else:
            write(0)
            (second,) = inverse_factors([matrix], 2)
            second_half(sweep, second)
            write(1)


def exchange(value, axes):
    return lax.all_to_all(value, axes, split_axis=0, concat_axis=0, tiled=True)


def sum_over(value, axes, members):
    return exchange(jnp.broadcast_to(value, (members, *value.shape)), axes).sum(axis=0)


def shards(species, start_basis):
    width, cells_z, cells_y = species.shape
    rank = start_basis.shape[1]
    tiles = len(lower_tiles(width // TILE))
    packed, high, low = pl.pallas_call(
        gram_kernel,
        out_shape=(
            jax.ShapeDtypeStruct((tiles * TILE, TILE), jnp.float32),
            jax.ShapeDtypeStruct((width, cells_z * cells_y), jnp.bfloat16),
            jax.ShapeDtypeStruct((width, cells_z * cells_y), jnp.bfloat16),
        ),
        compiler_params=PARAMS,
        name="gram",
    )(species)
    plane = ("row", "core")
    members = lax.axis_size(plane)
    part = exchange(packed.reshape(members, -1, TILE), plane).sum(axis=0)
    part = sum_over(part, ("zh", "zl"), lax.axis_size(("zh", "zl")))
    packed = exchange(jnp.broadcast_to(part, (members, *part.shape)), plane)
    core, basis = pl.pallas_call(
        basis_kernel,
        out_shape=(
            jax.ShapeDtypeStruct((rank, cells_z, cells_y), jnp.float32),
            jax.ShapeDtypeStruct((width, rank), jnp.float32),
        ),
        scratch_shapes=[
            pltpu.VMEM((width, width), jnp.bfloat16),
            pltpu.VMEM((width, width), jnp.bfloat16),
            pltpu.VMEM((ITERS + 1, 2, rank // 2, width), jnp.float32),
            pltpu.VMEM((ITERS, 2, rank // 2, width), jnp.float32),
            pltpu.VMEM((ITERS, rank // 2, width), jnp.float32),
        ],
        compiler_params=PARAMS,
        name="basis",
    )(packed.reshape(-1, TILE), start_basis, high, low)
    core = lax.all_to_all(core, "row", split_axis=0, concat_axis=2, tiled=True)
    return core, basis


def solution(mesh):
    rows, columns = mesh.devices.shape
    fine = Mesh(mesh.devices.reshape(rows, columns // 8, 4, 2), ("row", "zh", "zl", "core"))
    split = ("zh", "zl", "core")
    return jax.shard_map(
        shards,
        mesh=fine,
        in_specs=(P(None, split, "row"), P()),
        out_specs=(P("row", split, None), P()),
        check_vma=False,
    )
```

```python
import jax
import jax.numpy as jnp
from jax import lax
from jax.experimental import pallas as pl
from jax.experimental.pallas import tpu as pltpu
from jax.sharding import Mesh, PartitionSpec as P

ITERS = 2
TILE = 128
SUB = 8
NEAR = 2
NT = (((1,), (1,)), ((), ()))
NN = (((1,), (0,)), ((), ()))
PARAMS = pltpu.CompilerParams(vmem_limit_bytes=40 * 2**20)


def halves(value):
    high = value.astype(jnp.bfloat16)
    return high, (value - high.astype(jnp.float32)).astype(jnp.bfloat16)


def dot16(left, right, dims):
    return lax.dot_general(left, right, dims, preferred_element_type=jnp.float32)


def matmul(left, right, dims=NN):
    left_high, left_low = halves(left)
    right_high, right_low = halves(right)
    return dot16(left_high, right_high, dims) + (
        dot16(left_high, right_low, dims) + dot16(left_low, right_high, dims)
    )


def below_tiles(count):
    return [(i, j) for i in range(count) for j in range(i)]


def diagonal_places(count, i):
    half = TILE // 2
    first = len(below_tiles(count)) * TILE + i // 2 * 3 * half
    return pl.ds(first + i % 2 * 2 * half, half), pl.ds(first + half, half)


def gram_kernel(x_ref, packed_ref, high_ref, low_ref):
    width, cells_z, cells_y = x_ref.shape
    flat = x_ref.reshape(width * cells_z, cells_y)
    for z in range(cells_z):
        columns = pl.ds(z * cells_y, cells_y)
        high_ref[:, columns], low_ref[:, columns] = halves(
            flat[pl.ds(z, width, stride=cells_z), :]
        )
    count = width // TILE
    for step in range(count):
        rows, upto = pl.ds(step * TILE, TILE), pl.ds(0, (step + 1) * TILE)
        block = dot16(high_ref[rows, :], high_ref[upto, :], NT) + (
            dot16(high_ref[rows, :], low_ref[upto, :], NT)
            + dot16(low_ref[rows, :], high_ref[upto, :], NT)
        )
        for place, (a, b) in enumerate(below_tiles(count)):
            if a == step:
                packed_ref[pl.ds(place * TILE, TILE), :] = block[:, b * TILE : (b + 1) * TILE]
        tile = block[:, step * TILE :]
        top, bottom = tile[: TILE // 2], tile[TILE // 2 :]
        left = lax.broadcasted_iota(jnp.int32, top.shape, 1) < TILE // 2
        own, shared = diagonal_places(count, step)
        packed_ref[own, :] = jnp.where(left, top, bottom)
        packed_ref[shared, :] = jnp.where(left, packed_ref[shared, :], top) if step % 2 else bottom


def spread_row(tile, k):
    return jnp.broadcast_to(tile[k : k + 1, :], tile.shape)


def spread_column(tile, k):
    return jnp.broadcast_to(tile[:, k : k + 1], tile.shape)


def total_of(terms):
    while len(terms) > 1:
        terms = [sum(terms[i + 1 : i + 2], terms[i]) for i in range(0, len(terms), 2)]
    return terms[0]


def inverse_factors(matrices, depth):
    size = matrices[0].shape[0]
    count = size // SUB
    sub = lax.broadcasted_iota(jnp.int32, (SUB, size), 0)
    lane = lax.broadcasted_iota(jnp.int32, (SUB, size), 1)
    zero = jnp.zeros((SUB, size), jnp.float32)
    all_tiles = [[m[SUB * t : SUB * (t + 1), :] for t in range(count)] for m in matrices]
    all_done = [[] for _ in matrices]
    for t in range(0, count, depth):
        first, across = SUB * t, SUB * depth
        panel = (lane >= first) & (lane < first + across)
        for tiles, done in zip(all_tiles, all_done):
            own = range(depth)
            columns = [
                [spread_column(tiles[t + q], first + k) for k in range(across)] for q in own
            ]
            rest = [
                jnp.where(
                    panel, jnp.where(lane - first - SUB * q == sub, 1.0, 0.0), tiles[t + q]
                )
                for q in own
            ]
            forward, pivots, scales = list(rest), [None] * depth, [None] * depth
            for k in range(across):
                p, row = divmod(k, SUB)
                here = sub == row
                scale = 1.0 / spread_row(columns[p][k], row)
                factors = [columns[q][k] for q in own]
                factors[p] = jnp.where(here, 0.0, factors[p])
                if row:
                    forward[p] = jnp.where(sub >= row, rest[p], forward[p])
                    pivots[p] = jnp.where(here, columns[p][k], pivots[p])
                    scales[p] = jnp.where(here, scale, scales[p])
                else:
                    forward[p], pivots[p], scales[p] = rest[p], columns[p][k], scale
                for j in range(k + 1, across):
                    spread = spread_row(columns[p][j], row)
                    for q in own:
                        columns[q][j] = columns[q][j] - (factors[q] * spread) * scale
                spread = spread_row(rest[p], row)
                for q in own:
                    rest[q] = rest[q] - (factors[q] * spread) * scale
            solved = [rest[q] * scales[q] for q in own]
            rows = [spread_row(solved[k // SUB], k % SUB) for k in range(across)]
            near = t + depth
            far = min(near + NEAR, count)
            for i in range(near, far):
                change = [spread_column(tiles[i], first + k) * rows[k] for k in range(across)]
                tiles[i] = jnp.where(panel, 0.0, tiles[i]) - total_of(change)
            for q in own:
                kept = lane <= first + SUB * q + sub
                done.append(jnp.where(kept, forward[q] * lax.rsqrt(pivots[q]), 0.0))
            if far < count:
                right = [solved[i - t] if i - t in own else zero for i in range(count)]
                change = matmul(jnp.concatenate(tiles[far:], 0), jnp.concatenate(right, 0))
                for i in range(far, count):
                    place = SUB * (i - far)
                    tiles[i] = jnp.where(panel, 0.0, tiles[i]) - change[place : place + SUB]
    return [jnp.concatenate(done, axis=0) for done in all_done]


def basis_kernel(
    packed_ref, start_ref, high_ref, low_ref, core_ref, basis_ref, *scratch
):
    gram_high, gram_low, current_ref, applied_ref, rest_ref = scratch
    width = start_ref.shape[0]
    rank, cells_z, cells_y = core_ref.shape
    half = rank // 2
    count = width // TILE

    def keep(i, j, value):
        rows, columns = pl.ds(i * TILE, TILE), pl.ds(j * TILE, TILE)
        gram_high[rows, columns], gram_low[rows, columns] = halves(value)

    for place, (a, b) in enumerate(below_tiles(count)):
        tile = packed_ref[place * TILE : (place + 1) * TILE, :]
        keep(a, b, tile)
        keep(b, a, tile.T)
    for i in range(count):
        own, shared = (packed_ref[rows, :] for rows in diagonal_places(count, i))
        left = lax.broadcasted_iota(jnp.int32, own.shape, 1) < TILE // 2
        if i % 2:
            tile = jnp.concatenate([jnp.where(left, own, shared), own], axis=0)
        else:
            tile = jnp.concatenate([own, jnp.where(left, shared, own)], axis=0)
        row = lax.broadcasted_iota(jnp.int32, tile.shape, 0) < TILE // 2
        column = lax.broadcasted_iota(jnp.int32, tile.shape, 1) < TILE // 2
        missing = (column if i % 2 else row) & (row != column)
        keep(i, i, jnp.where(missing, tile.T, tile))

    def times_gram(sweep, part):
        high, low = halves(current_ref[sweep, part])
        applied_ref[sweep, part] = dot16(high, gram_high[...], NN) + (
            dot16(high, gram_low[...], NN) + dot16(low, gram_high[...], NN)
        )

    def inner(sweep, left, right):
        return matmul(applied_ref[sweep, left], applied_ref[sweep, right], NT)

    def first_half(sweep, inverse):
        current_ref[sweep + 1, 0] = matmul(inverse, applied_ref[sweep, 0])

    def second_matrix(sweep, inverse):
        below = matmul(inner(sweep, 1, 0), inverse, NT)
        rest_ref[sweep] = applied_ref[sweep, 1] - matmul(below, current_ref[sweep + 1, 0])
        return inner(sweep, 1, 1) - matmul(below, below, NT)

    def second_half(sweep, inverse):
        current_ref[sweep + 1, 1] = matmul(inverse, rest_ref[sweep])

    def write(part):
        value = current_ref[ITERS, part]
        basis_ref[:, part * half : (part + 1) * half] = value.T
        high, low = halves(value)
        flat = core_ref.reshape(rank * cells_z, cells_y)
        for z in range(0, cells_z, 2):
            columns = pl.ds(z * cells_y, 2 * cells_y)
            block = dot16(high, high_ref[:, columns], NN) + (
                dot16(high, low_ref[:, columns], NN) + dot16(low, high_ref[:, columns], NN)
            )
            for q in range(2):
                rows = pl.ds(part * half * cells_z + z + q, half, stride=cells_z)
                flat[rows, :] = block[:, q * cells_y : (q + 1) * cells_y]

    for part in range(2):
        current_ref[0, part] = start_ref[:, part * half : (part + 1) * half].T
        times_gram(0, part)
    (inverse,) = inverse_factors([inner(0, 0, 0)], 2)
    for sweep in range(ITERS):
        first_half(sweep, inverse)
        matrix = second_matrix(sweep, inverse)
        if sweep + 1 < ITERS:
            times_gram(sweep + 1, 0)
            second, inverse = inverse_factors([matrix, inner(sweep + 1, 0, 0)], 2)
            second_half(sweep, second)
            times_gram(sweep + 1, 1)
        else:
            write(0)
            (second,) = inverse_factors([matrix], 2)
            second_half(sweep, second)
            write(1)


def exchange(value, axes):
    return lax.all_to_all(value, axes, split_axis=0, concat_axis=0, tiled=True)


def sum_over(value, axes, members):
    return exchange(jnp.broadcast_to(value, (members, *value.shape)), axes).sum(axis=0)


def shards(species, start_basis):
    width, cells_z, cells_y = species.shape
    rank = start_basis.shape[1]
    tiles = width // TILE
    packed_rows = (len(below_tiles(tiles)) + tiles * 3 // 4) * TILE
    packed, high, low = pl.pallas_call(
        gram_kernel,
        out_shape=(
            jax.ShapeDtypeStruct((packed_rows, TILE), jnp.float32),
            jax.ShapeDtypeStruct((width, cells_z * cells_y), jnp.bfloat16),
            jax.ShapeDtypeStruct((width, cells_z * cells_y), jnp.bfloat16),
        ),
        compiler_params=PARAMS,
        name="gram",
    )(species)
    plane = ("row", "core")
    members = lax.axis_size(plane)
    part = exchange(packed.reshape(members, -1, 4, TILE), plane).sum(axis=0)
    part = sum_over(part, ("zh", "zl"), lax.axis_size(("zh", "zl")))
    packed = exchange(jnp.broadcast_to(part, (members, *part.shape)), plane)
    core, basis = pl.pallas_call(
        basis_kernel,
        out_shape=(
            jax.ShapeDtypeStruct((rank, cells_z, cells_y), jnp.float32),
            jax.ShapeDtypeStruct((width, rank), jnp.float32),
        ),
        scratch_shapes=[
            pltpu.VMEM((width, width), jnp.bfloat16),
            pltpu.VMEM((width, width), jnp.bfloat16),
            pltpu.VMEM((ITERS + 1, 2, rank // 2, width), jnp.float32),
            pltpu.VMEM((ITERS, 2, rank // 2, width), jnp.float32),
            pltpu.VMEM((ITERS, rank // 2, width), jnp.float32),
        ],
        compiler_params=PARAMS,
        name="basis",
    )(packed.reshape(-1, TILE), start_basis, high, low)
    core = lax.all_to_all(core, "row", split_axis=0, concat_axis=2, tiled=True)
    return core, basis


def solution(mesh):
    rows, columns = mesh.devices.shape
    fine = Mesh(mesh.devices.reshape(rows, columns // 8, 4, 2), ("row", "zh", "zl", "core"))
    split = ("zh", "zl", "core")
    return jax.shard_map(
        shards,
        mesh=fine,
        in_specs=(P(None, split, "row"), P()),
        out_specs=(P("row", split, None), P()),
        check_vma=False,
    )
```

```python
import jax
import jax.numpy as jnp
from jax import lax
from jax.experimental import pallas as pl
from jax.experimental.pallas import tpu as pltpu
from jax.sharding import Mesh, PartitionSpec as P

ITERS = 2
TILE = 128
SUB = 8
NEAR = 2
NT = (((1,), (1,)), ((), ()))
NN = (((1,), (0,)), ((), ()))
PARAMS = pltpu.CompilerParams(vmem_limit_bytes=40 * 2**20)


def halves(value):
    high = value.astype(jnp.bfloat16)
    return high, (value - high.astype(jnp.float32)).astype(jnp.bfloat16)


def dot16(left, right, dims):
    return lax.dot_general(left, right, dims, preferred_element_type=jnp.float32)


def matmul(left, right, dims=NN):
    left_high, left_low = halves(left)
    right_high, right_low = halves(right)
    return dot16(left_high, right_high, dims) + (
        dot16(left_high, right_low, dims) + dot16(left_low, right_high, dims)
    )


def below_tiles(count):
    return [(i, j) for i in range(count) for j in range(i)]


def diagonal_places(count, i):
    half = TILE // 2
    first = len(below_tiles(count)) * TILE + i // 2 * 3 * half
    return pl.ds(first + i % 2 * 2 * half, half), pl.ds(first + half, half)


def gram_kernel(x_ref, packed_ref, high_ref, low_ref):
    width, cells_z, cells_y = x_ref.shape
    flat = x_ref.reshape(width * cells_z, cells_y)
    for z in range(cells_z):
        columns = pl.ds(z * cells_y, cells_y)
        high_ref[:, columns], low_ref[:, columns] = halves(
            flat[pl.ds(z, width, stride=cells_z), :]
        )
    count, side = width // TILE, 2 * TILE
    for i, j in below_tiles(width // side) + [(i, i) for i in range(width // side)]:
        rows, columns = pl.ds(i * side, side), pl.ds(j * side, side)
        block = dot16(high_ref[rows, :], high_ref[columns, :], NT)
        cross = dot16(high_ref[rows, :], low_ref[columns, :], NT)
        if i == j:
            block = block + (cross + cross.T)
        else:
            block = block + (cross + dot16(low_ref[rows, :], high_ref[columns, :], NT))
        for place, (a, b) in enumerate(below_tiles(count)):
            if (a // 2, b // 2) == (i, j):
                p, q = a % 2 * TILE, b % 2 * TILE
                packed_ref[pl.ds(place * TILE, TILE), :] = block[p : p + TILE, q : q + TILE]
        if i != j:
            continue
        half = TILE // 2
        left = lax.broadcasted_iota(jnp.int32, (half, TILE), 1) < half
        first, second = block[:TILE, :TILE], block[TILE:, TILE:]
        own, shared = diagonal_places(count, 2 * i)
        packed_ref[own, :] = jnp.where(left, first[:half], first[half:])
        packed_ref[shared, :] = jnp.where(left, first[half:], second[:half])
        own, shared = diagonal_places(count, 2 * i + 1)
        packed_ref[own, :] = jnp.where(left, second[:half], second[half:])


def spread_row(tile, k):
    return jnp.broadcast_to(tile[k : k + 1, :], tile.shape)


def spread_column(tile, k):
    return jnp.broadcast_to(tile[:, k : k + 1], tile.shape)


def total_of(terms):
    while len(terms) > 1:
        terms = [sum(terms[i + 1 : i + 2], terms[i]) for i in range(0, len(terms), 2)]
    return terms[0]


def inverse_factors(matrices, depth):
    size = matrices[0].shape[0]
    count = size // SUB
    sub = lax.broadcasted_iota(jnp.int32, (SUB, size), 0)
    lane = lax.broadcasted_iota(jnp.int32, (SUB, size), 1)
    zero = jnp.zeros((SUB, size), jnp.float32)
    all_tiles = [[m[SUB * t : SUB * (t + 1), :] for t in range(count)] for m in matrices]
    all_done = [[] for _ in matrices]
    for t in range(0, count, depth):
        first, across = SUB * t, SUB * depth
        panel = (lane >= first) & (lane < first + across)
        for tiles, done in zip(all_tiles, all_done):
            own = range(depth)
            columns = [
                [spread_column(tiles[t + q], first + k) for k in range(across)] for q in own
            ]
            rest = [
                jnp.where(
                    panel, jnp.where(lane - first - SUB * q == sub, 1.0, 0.0), tiles[t + q]
                )
                for q in own
            ]
            forward, pivots, scales = list(rest), [None] * depth, [None] * depth
            for k in range(across):
                p, row = divmod(k, SUB)
                here = sub == row
                scale = 1.0 / spread_row(columns[p][k], row)
                factors = [columns[q][k] for q in own]
                factors[p] = jnp.where(here, 0.0, factors[p])
                if row:
                    forward[p] = jnp.where(sub >= row, rest[p], forward[p])
                    pivots[p] = jnp.where(here, columns[p][k], pivots[p])
                    scales[p] = jnp.where(here, scale, scales[p])
                else:
                    forward[p], pivots[p], scales[p] = rest[p], columns[p][k], scale
                for j in range(k + 1, across):
                    spread = spread_row(columns[p][j], row)
                    for q in own:
                        columns[q][j] = columns[q][j] - (factors[q] * spread) * scale
                spread = spread_row(rest[p], row)
                for q in own:
                    rest[q] = rest[q] - (factors[q] * spread) * scale
            solved = [rest[q] * scales[q] for q in own]
            rows = [spread_row(solved[k // SUB], k % SUB) for k in range(across)]
            near = t + depth
            far = min(near + NEAR, count)
            for i in range(near, far):
                change = [spread_column(tiles[i], first + k) * rows[k] for k in range(across)]
                tiles[i] = jnp.where(panel, 0.0, tiles[i]) - total_of(change)
            for q in own:
                kept = lane <= first + SUB * q + sub
                done.append(jnp.where(kept, forward[q] * lax.rsqrt(pivots[q]), 0.0))
            if far < count:
                right = [solved[i - t] if i - t in own else zero for i in range(count)]
                change = matmul(jnp.concatenate(tiles[far:], 0), jnp.concatenate(right, 0))
                for i in range(far, count):
                    place = SUB * (i - far)
                    tiles[i] = jnp.where(panel, 0.0, tiles[i]) - change[place : place + SUB]
    return [jnp.concatenate(done, axis=0) for done in all_done]


def basis_kernel(
    packed_ref, start_ref, high_ref, low_ref, core_ref, basis_ref, *scratch
):
    gram_high, gram_low, current_ref, applied_ref, rest_ref = scratch
    width = start_ref.shape[0]
    rank, cells_z, cells_y = core_ref.shape
    half = rank // 2
    count = width // TILE

    def keep(i, j, value):
        rows, columns = pl.ds(i * TILE, TILE), pl.ds(j * TILE, TILE)
        gram_high[rows, columns], gram_low[rows, columns] = halves(value)

    for place, (a, b) in enumerate(below_tiles(count)):
        tile = packed_ref[place * TILE : (place + 1) * TILE, :]
        keep(a, b, tile)
        keep(b, a, tile.T)
    for i in range(count):
        own, shared = (packed_ref[rows, :] for rows in diagonal_places(count, i))
        left = lax.broadcasted_iota(jnp.int32, own.shape, 1) < TILE // 2
        if i % 2:
            tile = jnp.concatenate([jnp.where(left, own, shared), own], axis=0)
        else:
            tile = jnp.concatenate([own, jnp.where(left, shared, own)], axis=0)
        row = lax.broadcasted_iota(jnp.int32, tile.shape, 0) < TILE // 2
        column = lax.broadcasted_iota(jnp.int32, tile.shape, 1) < TILE // 2
        missing = (column if i % 2 else row) & (row != column)
        keep(i, i, jnp.where(missing, tile.T, tile))

    def times_gram(sweep, part):
        high, low = halves(current_ref[sweep, part])
        applied_ref[sweep, part] = dot16(high, gram_high[...], NN) + (
            dot16(high, gram_low[...], NN) + dot16(low, gram_high[...], NN)
        )

    def inner(sweep, left, right):
        return matmul(applied_ref[sweep, left], applied_ref[sweep, right], NT)

    def first_half(sweep, inverse):
        current_ref[sweep + 1, 0] = matmul(inverse, applied_ref[sweep, 0])

    def second_matrix(sweep, inverse):
        below = matmul(inner(sweep, 1, 0), inverse, NT)
        rest_ref[sweep] = applied_ref[sweep, 1] - matmul(below, current_ref[sweep + 1, 0])
        return inner(sweep, 1, 1) - matmul(below, below, NT)

    def second_half(sweep, inverse):
        current_ref[sweep + 1, 1] = matmul(inverse, rest_ref[sweep])

    def write(part):
        value = current_ref[ITERS, part]
        basis_ref[:, part * half : (part + 1) * half] = value.T
        high, low = halves(value)
        flat = core_ref.reshape(rank * cells_z, cells_y)
        for z in range(0, cells_z, 2):
            columns = pl.ds(z * cells_y, 2 * cells_y)
            block = dot16(high, high_ref[:, columns], NN) + (
                dot16(high, low_ref[:, columns], NN) + dot16(low, high_ref[:, columns], NN)
            )
            for q in range(2):
                rows = pl.ds(part * half * cells_z + z + q, half, stride=cells_z)
                flat[rows, :] = block[:, q * cells_y : (q + 1) * cells_y]

    for part in range(2):
        current_ref[0, part] = start_ref[:, part * half : (part + 1) * half].T
        times_gram(0, part)
    (inverse,) = inverse_factors([inner(0, 0, 0)], 2)
    for sweep in range(ITERS):
        first_half(sweep, inverse)
        matrix = second_matrix(sweep, inverse)
        if sweep + 1 < ITERS:
            times_gram(sweep + 1, 0)
            second, inverse = inverse_factors([matrix, inner(sweep + 1, 0, 0)], 2)
            second_half(sweep, second)
            times_gram(sweep + 1, 1)
        else:
            write(0)
            (second,) = inverse_factors([matrix], 2)
            second_half(sweep, second)
            write(1)


def exchange(value, axes):
    return lax.all_to_all(value, axes, split_axis=0, concat_axis=0, tiled=True)


def sum_over(value, axes, members):
    return exchange(jnp.broadcast_to(value, (members, *value.shape)), axes).sum(axis=0)


def shards(species, start_basis):
    width, cells_z, cells_y = species.shape
    rank = start_basis.shape[1]
    tiles = width // TILE
    packed_rows = (len(below_tiles(tiles)) + tiles * 3 // 4) * TILE
    packed, high, low = pl.pallas_call(
        gram_kernel,
        out_shape=(
            jax.ShapeDtypeStruct((packed_rows, TILE), jnp.float32),
            jax.ShapeDtypeStruct((width, cells_z * cells_y), jnp.bfloat16),
            jax.ShapeDtypeStruct((width, cells_z * cells_y), jnp.bfloat16),
        ),
        compiler_params=PARAMS,
        name="gram",
    )(species)
    plane = ("row", "core")
    members = lax.axis_size(plane)
    part = exchange(packed.reshape(members, -1, 4, TILE), plane).sum(axis=0)
    part = sum_over(part, ("zh", "zl"), lax.axis_size(("zh", "zl")))
    packed = exchange(jnp.broadcast_to(part, (members, *part.shape)), plane)
    core, basis = pl.pallas_call(
        basis_kernel,
        out_shape=(
            jax.ShapeDtypeStruct((rank, cells_z, cells_y), jnp.float32),
            jax.ShapeDtypeStruct((width, rank), jnp.float32),
        ),
        scratch_shapes=[
            pltpu.VMEM((width, width), jnp.bfloat16),
            pltpu.VMEM((width, width), jnp.bfloat16),
            pltpu.VMEM((ITERS + 1, 2, rank // 2, width), jnp.float32),
            pltpu.VMEM((ITERS, 2, rank // 2, width), jnp.float32),
            pltpu.VMEM((ITERS, rank // 2, width), jnp.float32),
        ],
        compiler_params=PARAMS,
        name="basis",
    )(packed.reshape(-1, TILE), start_basis, high, low)
    core = lax.all_to_all(core, "row", split_axis=0, concat_axis=2, tiled=True)
    return core, basis


def solution(mesh):
    rows, columns = mesh.devices.shape
    fine = Mesh(mesh.devices.reshape(rows, columns // 8, 4, 2), ("row", "zh", "zl", "core"))
    split = ("zh", "zl", "core")
    return jax.shard_map(
        shards,
        mesh=fine,
        in_specs=(P(None, split, "row"), P()),
        out_specs=(P("row", split, None), P()),
        check_vma=False,
    )
```
